256 devices in a mesh: member: 8 (over y, core), dp: 16 (over z_lo, x), owner: 2 (over z_hi).
Axes of the slice: x: 4, y: 4, z: 8 (z_hi: 2, z_lo: 4; z = z_hi * 4 + z_lo), core: 2. Of those that a mesh axis runs over, the one named last changes fastest.
Arguments:
- factor_rows: bfloat16 [2, 32768, 8192], P('owner', ('member', 'dp')), parts along dimension 1, may hold values from -50 to 50, as said below
- feature_order: int32 [2, 8192], P('owner'), may hold values from 0 to 8191, each once within a row
- gradients: bfloat16 [2, 8192, 16384], P('owner', None, ('member', 'dp')), parts along dimension 2, may hold values from -6 to 6
Outputs:
- preconditioned: bfloat16 [2, 8192, 16384], P('owner', None, ('member', 'dp')), parts along dimension 2
The draws below stay inside these ranges and needn't reach their ends.
There are 8 independent parts, one for each index of `member`. The reference program is written for one: setup_inputs(seed, part) draws one part's arguments, and reference() takes and returns one part's arrays. A program takes and returns all parts, laid end to end along the dimension named above; an argument that names none is the same for every part. Nothing has to cross between parts.
Inputs may be any that keep to these rules, and one draw needn't show every extreme that they name: `factor_rows`: real-valued data, column scales differing across hidden units. `feature_order`: each row is a permutation of 0 to 8191.
All inputs are finite; a program needn't handle non-finite values. Where the reference program divides by a largest or mean magnitude, that divisor is 1e-20 or more.
Results may differ from the reference program's by a relative error of at most 0.005.
Values may be sent and summed in bfloat16 or wider, within the bound.
No kernel may reach another device: no remote copies, remote signals or barrier semaphores. Data moves between devices by JAX's collectives and lax.ppermute only.
A program may use at most 128 MiB of HBM per device.

```python
import jax
import jax.numpy as jnp
from jax import lax

D = 2048
FF = 8192
BLK = 512
NS_STEPS = 12
TOKENS = 4096


def draw_factor_rows(key, part):
    key = jax.random.fold_in(key, 11)
    key_scale, key_base = jax.random.split(key, 2)
    scales = jnp.exp(jax.random.uniform(key_scale, (2, 1, FF), jnp.float32) * jnp.log(10.0))
    base = jnp.clip(jax.random.normal(key_base, (2, TOKENS, FF), jnp.float32), -5.0, 5.0)
    values = base * scales
    return values.astype(jnp.bfloat16)


def levels(own_key, shape, cuts, smallest, high):
    level, own = 1.0, jax.random.fold_in(own_key, 6)
    for dim, shards_of in cuts:
        draws = jnp.exp(jax.random.uniform(jax.random.fold_in(own, dim), (shards_of,), jnp.float32, smallest / len(cuts), high / len(cuts)))
        level = level * jnp.repeat(draws, shape[dim] // shards_of).reshape([-1 if axis == dim else 1 for axis in range(len(shape))])
    return level


def centred(rng, dims, deviation, most, pieces=(), held_as=jnp.bfloat16):
    drawn = deviation * jax.random.normal(rng, dims, jnp.float32)
    if pieces:
        drawn = drawn * levels(rng, dims, pieces, -0.22, 0.18)
    return jnp.clip(drawn, -most, most).astype(held_as)


def setup_inputs(seed: int = 0, part: int = 0) -> dict:
    splits = jax.random.split(jax.random.key(seed), 4)
    own_keys = jax.random.split(jax.random.fold_in(splits[3], part), 4)
    factor_rows = draw_factor_rows(jax.random.fold_in(jax.random.fold_in(splits[3], part), 71), part)
    feature_order = jax.vmap(lambda own: jax.random.permutation(own, FF))(jax.random.split(splits[1], 2)).reshape((2, FF)).astype(jnp.int32)
    gradients = centred(own_keys[2], (2, FF, D), 1.0, 6.0, ((0, 2), (2, 16)))
    return {"factor_rows": factor_rows, "feature_order": feature_order, "gradients": gradients}


DAMPING = 1e-3


def newton_inverse(damped):
    identity = jnp.eye(damped.shape[0], dtype=jnp.float32)
    step_scale = 1.0 / jnp.max(jnp.sum(jnp.abs(damped), axis=1))
    approx = step_scale * identity
    for iteration in range(NS_STEPS):
        product = jnp.dot(damped, approx, precision=lax.Precision.HIGHEST)
        approx = jnp.dot(approx, 2.0 * identity - product, precision=lax.Precision.HIGHEST)
    return approx


def reference(factor_rows, feature_order, gradients):
    outputs = []
    for factor_side in range(2):
        data_rows = factor_rows[factor_side]
        feature_perm = feature_order[factor_side]
        grad_rows = gradients[factor_side]

        def one_block(block_index):
            columns = lax.dynamic_slice_in_dim(feature_perm, block_index * BLK, BLK)
            selected = jnp.take(data_rows, columns, axis=1)
            covariance = jnp.dot(selected.T, selected, preferred_element_type=jnp.float32) / TOKENS
            damped = covariance + DAMPING * jnp.eye(BLK, dtype=jnp.float32)
            inverse = newton_inverse(damped).astype(jnp.bfloat16)
            picked = jnp.take(grad_rows, columns, axis=0)
            return jnp.dot(inverse, picked, preferred_element_type=jnp.float32).astype(jnp.bfloat16)

        blocks = lax.map(one_block, jnp.arange(FF // BLK, dtype=jnp.int32))
        restored = jnp.zeros((FF, D), jnp.bfloat16).at[feature_perm].set(blocks.reshape(FF, D))
        outputs.append(restored)
    return jnp.stack(outputs)
```

```python
import functools

import jax
import jax.numpy as jnp
from jax import lax
from jax.experimental import pallas as pl
from jax.experimental.pallas import tpu as pltpu
from jax.sharding import PartitionSpec as P

BLK = 512
NS_STEPS = 12
DAMPING = 0.001
TILE = 128
LANES = 128
SIDE = BLK // TILE
UPPER = [(r, c) for r in range(SIDE) for c in range(r + 1, SIDE)]
DIAGONAL = [(r, r + 1) for r in range(0, SIDE, 2)]
TAIL = (len(UPPER) + len(DIAGONAL)) * TILE
PACKED = TAIL + 16
RING = 4
LINE = 4
UNROLL = 64
PHASES = (3, 2, 1, 0)

VMEM = pl.BlockSpec(memory_space=pltpu.VMEM)
SMEM = pl.BlockSpec(memory_space=pltpu.SMEM)
ANY = pl.BlockSpec(memory_space=pl.ANY)
PARAMS = pltpu.CompilerParams(vmem_limit_bytes=48 * 1024 * 1024)


def ring_shift(value, step):
    pairs = [
        (z * RING + x, z * RING + (x + step) % RING) for z in range(LINE) for x in range(RING)
    ]
    return lax.ppermute(value, "dp", pairs)


def line_swap(value, mask):
    pairs = [(z * RING + x, (z ^ mask) * RING + x) for z in range(LINE) for x in range(RING)]
    return lax.ppermute(value, "dp", pairs)


def block_start(phase, offset):
    place = lax.axis_index("dp")
    z = lax.div(place, RING)
    x = lax.rem(place, RING)
    block = lax.bitwise_xor(z, phase) * RING + lax.rem(x + offset, RING)
    return block * BLK


def gather_rows(order, start, sources, targets):
    def step(group, carry):
        first = pl.multiple_of(group * UNROLL, UNROLL)
        for inner in range(UNROLL):
            row = order[0, start + first + inner]
            for source, target in zip(sources, targets):
                target[pl.ds(first + inner, 1), :] = source[pl.ds(row, 1), :]
        return carry

    lax.fori_loop(0, BLK // UNROLL, step, 0)


def pick_columns_kernel(phases, order, rows, *refs):
    outs, turned, picked = refs[-RING - 4 : -4], refs[-4:-2], refs[-2:]
    width = 256
    for first in range(0, rows.shape[1], width):
        part = rows[:, first : first + width].astype(jnp.float32).T
        for half, target in enumerate(turned):
            target[first : first + width, :] = part[:, half * LANES : (half + 1) * LANES]
    for offset in range(RING):
        for place, phase in enumerate(phases):
            gather_rows(order, block_start(phase, offset), turned, picked)
            for half, source in enumerate(picked):
                outs[offset][
                    place * BLK : (place + 1) * BLK, half * LANES : (half + 1) * LANES
                ] = source[...].astype(jnp.bfloat16)


def pick_columns(phases, order, rows, after=()):
    tokens, features = rows.shape
    return pl.pallas_call(
        functools.partial(pick_columns_kernel, phases),
        out_shape=[jax.ShapeDtypeStruct((len(phases) * BLK, tokens), jnp.bfloat16)] * RING,
        in_specs=[SMEM, VMEM] + [ANY] * len(after),
        out_specs=[VMEM] * RING,
        scratch_shapes=[pltpu.VMEM((features, LANES), jnp.float32)] * 2
        + [pltpu.VMEM((BLK, LANES), jnp.float32)] * 2,
        compiler_params=PARAMS,
        name="pick_columns",
    )(order, rows, *after)


def pick_grads_kernel(order, grads, *refs):
    outs, (wide, picked) = refs[-2 - RING : -2], refs[-2:]
    wide[...] = grads[...].astype(jnp.float32)
    for place, phase in enumerate(PHASES):
        for offset in range(RING):
            gather_rows(order, block_start(phase, offset), [wide], [picked])
            outs[offset][place * BLK : (place + 1) * BLK, :] = picked[...].astype(jnp.bfloat16)


def pick_grads(order, grads, after=()):
    features, columns = grads.shape
    return pl.pallas_call(
        pick_grads_kernel,
        out_shape=[jax.ShapeDtypeStruct((LINE * BLK, columns), jnp.bfloat16)] * RING,
        in_specs=[SMEM, VMEM] + [ANY] * len(after),
        out_specs=[VMEM] * RING,
        scratch_shapes=[
            pltpu.VMEM((features, columns), jnp.float32),
            pltpu.VMEM((BLK, columns), jnp.float32),
        ],
        compiler_params=PARAMS,
        name="pick_grads",
    )(order, grads, *after)


def tile_indices():
    rows = lax.broadcasted_iota(jnp.int32, (TILE, TILE), 0)
    columns = lax.broadcasted_iota(jnp.int32, (TILE, TILE), 1)
    return rows, columns


def pack(tile_at):
    rows, columns = tile_indices()
    parts = [tile_at(r, c) for r, c in UPPER]
    tails = []
    for first, second in DIAGONAL:
        other = tile_at(second, second)
        parts.append(jnp.where(columns >= rows, tile_at(first, first), other))
        tails.append(jnp.sum(jnp.where(rows == columns, other, 0.0), axis=0, keepdims=True))
    tails.append(jnp.zeros((PACKED - TAIL - len(tails), TILE), jnp.float32))
    return parts + [jnp.concatenate(tails, axis=0)]


def unpack(packed, target):
    rows, columns = tile_indices()

    def store(r, c, value):
        target[r * TILE : (r + 1) * TILE, c * TILE : (c + 1) * TILE] = value.astype(target.dtype)

    for place, (r, c) in enumerate(UPPER):
        value = packed(place * TILE, TILE)
        store(r, c, value)
        store(c, r, value.T)
    tails = packed(TAIL, PACKED - TAIL)
    for place, (first, second) in enumerate(DIAGONAL):
        value = packed((len(UPPER) + place) * TILE, TILE)
        turned = value.T
        store(first, first, jnp.where(columns >= rows, value, turned))
        upper = jnp.where(columns > rows, turned, tails[place : place + 1, :])
        store(second, second, jnp.where(columns < rows, value, upper))


def store_parts(out, parts, extra=()):
    start = 0
    for part in parts:
        stop = start + part.shape[0]
        for other in extra:
            part = part + other[start:stop, :]
        out[start:stop, :] = part.astype(out.dtype)
        start = stop


def products_kernel(count, adds, *refs):
    pieces, extra = refs[:RING], refs[RING : RING + adds]
    outs, joined = refs[-1 - count : -1], refs[-1]
    tokens = pieces[0].shape[1]
    for index, out in enumerate(outs):
        for place, piece in enumerate(pieces):
            joined[:, place * tokens : (place + 1) * tokens] = piece[
                index * BLK : (index + 1) * BLK, :
            ]
        strips = [
            lax.dot_general(
                joined[r * TILE : (r + 1) * TILE, :],
                joined[r * TILE :, :],
                (((1,), (1,)), ((), ())),
                preferred_element_type=jnp.float32,
            )
            for r in range(SIDE)
        ]
        store_parts(out, pack(lambda r, c: strips[r][:, (c - r) * TILE : (c - r + 1) * TILE]), extra)


def products(pieces, *extra, after=()):
    tokens = pieces[0].shape[1]
    count = pieces[0].shape[0] // BLK
    return pl.pallas_call(
        functools.partial(products_kernel, count, len(extra)),
        out_shape=[jax.ShapeDtypeStruct((PACKED, TILE), jnp.float32)] * count,
        in_specs=[VMEM] * (RING + len(extra)) + [ANY] * len(after),
        out_specs=[VMEM] * count,
        scratch_shapes=[pltpu.VMEM((BLK, RING * tokens), jnp.bfloat16)],
        compiler_params=PARAMS,
        name="products",
    )(*pieces, *extra, *after)


def halves(value):
    high = value.astype(jnp.bfloat16)
    low = (value - high.astype(jnp.float32)).astype(jnp.bfloat16)
    return high, low


def dot(left, right):
    return jnp.dot(left, right, preferred_element_type=jnp.float32)


def dot3(left, right):
    left_high, left_low = left
    right_high, right_low = right
    return dot(left_high, right_high) + (dot(left_high, right_low) + dot(left_low, right_high))


def newton_kernel(total, own, sibling, far, out, damped):
    rows = lax.broadcasted_iota(jnp.int32, (BLK, BLK), 0)
    columns = lax.broadcasted_iota(jnp.int32, (BLK, BLK), 1)
    identity = jnp.where(rows == columns, 1.0, 0.0).astype(jnp.float32)
    def packed(start, size):
        part = slice(start, start + size)
        return (own[part, :] + sibling[part, :] + far[part, :]) / float(total)

    unpack(packed, damped)
    matrix = damped[...] + DAMPING * identity
    scale = 1.0 / jnp.max(jnp.sum(jnp.abs(matrix), axis=1, keepdims=True), axis=0, keepdims=True)
    matrix_parts = halves(matrix)
    approx = scale * (2.0 * identity - scale * matrix)

    def step(iteration, current):
        parts = halves(current)
        residual = identity - dot3(matrix_parts, parts)
        return current + dot3(parts, halves(residual))

    approx = lax.fori_loop(1, NS_STEPS, step, approx)
    store_parts(
        out,
        pack(lambda r, c: approx[r * TILE : (r + 1) * TILE, c * TILE : (c + 1) * TILE]),
    )


def newton(total, own, sibling, far):
    return pl.pallas_call(
        functools.partial(newton_kernel, total),
        out_shape=jax.ShapeDtypeStruct((PACKED, TILE), jnp.bfloat16),
        in_specs=[VMEM] * 3,
        out_specs=VMEM,
        scratch_shapes=[pltpu.VMEM((BLK, BLK), jnp.float32)],
        compiler_params=PARAMS,
        name="newton",
    )(own, sibling, far)


def apply_kernel(places, waits, *refs):
    count = len(places)
    inverses, pieces = refs[:count], refs[count : count + RING]
    outs, (full, joined) = refs[count + RING + waits : -2], refs[-2:]
    columns = pieces[0].shape[1]
    for index, (place, inverse) in enumerate(zip(places, inverses)):
        unpack(lambda start, size: inverse[start : start + size, :].astype(jnp.float32), full)
        for offset, piece in enumerate(pieces):
            joined[:, offset * columns : (offset + 1) * columns] = piece[
                place * BLK : (place + 1) * BLK, :
            ]
        result = dot(full[...], joined[...]).astype(jnp.bfloat16)
        for offset in range(RING):
            outs[offset][index * BLK : (index + 1) * BLK, :] = result[
                :, offset * columns : (offset + 1) * columns
            ]


def apply(places, inverses, pieces, after=()):
    columns = pieces[0].shape[1]
    shapes = [jax.ShapeDtypeStruct((len(places) * BLK, columns), jnp.bfloat16)] * RING
    return pl.pallas_call(
        functools.partial(apply_kernel, places, len(after)),
        out_shape=shapes,
        in_specs=[VMEM] * (RING + len(places)) + [ANY] * len(after),
        out_specs=[VMEM] * len(shapes),
        scratch_shapes=[
            pltpu.VMEM((BLK, BLK), jnp.bfloat16),
            pltpu.VMEM((BLK, RING * columns), jnp.bfloat16),
        ],
        compiler_params=PARAMS,
        name="apply",
    )(*inverses, *pieces, *after)


def put_back_kernel(groups, last, order, *refs):
    pieces, refs = refs[: RING * len(groups)], refs[RING * len(groups) :]
    if last:
        before, out, wide, held = refs
        wide[...] = before[...]
    else:
        wide, held = refs
    for group, places in enumerate(groups):
        for index, place in enumerate(places):
            for offset in range(RING):
                start = block_start(PHASES[place], offset)
                piece = pieces[group * RING + offset]
                held[...] = piece[index * BLK : (index + 1) * BLK, :].astype(jnp.float32)

                def step(batch, carry):
                    first = pl.multiple_of(batch * UNROLL, UNROLL)
                    for inner in range(UNROLL):
                        row = order[0, start + first + inner]
                        wide[pl.ds(row, 1), :] = held[pl.ds(first + inner, 1), :]
                    return carry

                lax.fori_loop(0, BLK // UNROLL, step, 0)
    if last:
        out[...] = wide[...].astype(jnp.bfloat16)


def put_back(order, groups, pieces, before=None):
    columns = pieces[0].shape[1]
    features = order.shape[1]
    last = before is not None
    wide = pltpu.VMEM((features, columns), jnp.float32)
    held = pltpu.VMEM((BLK, columns), jnp.float32)
    return pl.pallas_call(
        functools.partial(put_back_kernel, groups, last),
        out_shape=jax.ShapeDtypeStruct(
            (features, columns), jnp.bfloat16 if last else jnp.float32
        ),
        in_specs=[SMEM] + [VMEM] * (len(pieces) + last),
        out_specs=VMEM,
        scratch_shapes=[wide, held] if last else [held],
        compiler_params=PARAMS,
        name="put_back",
    )(order, *pieces, *([before] if last else []))


def exchange(pieces, sign):
    return [pieces[0]] + [ring_shift(pieces[k], sign * k) for k in range(1, RING)]


def shards(factor_rows, feature_order, gradients):
    rows = factor_rows[0]
    grads = gradients[0]
    total = rows.shape[0] * lax.axis_size("dp")

    order = feature_order
    picked_0 = pick_columns(PHASES[:1], order, rows)
    picked_1 = pick_columns(PHASES[1:2], order, rows, after=picked_0[:1])
    arrived_0 = exchange(picked_0, 1)
    arrived_1 = exchange(picked_1, 1)
    (partial_0,) = products(arrived_0, after=picked_1[:1])
    from_3 = line_swap(partial_0, 1)
    picked_2 = pick_columns(PHASES[2:3], order, rows, after=[partial_0])
    (partial_1,) = products(arrived_1, from_3, after=picked_2[:1])
    from_2 = line_swap(partial_1, 2)
    arrived_2 = exchange(picked_2, 1)
    picked_3 = pick_columns(PHASES[3:], order, rows, after=[partial_1])
    (partial_2,) = products(arrived_2, after=picked_3[:1])
    partial_2, picked_3 = lax.optimization_barrier((partial_2, picked_3))
    from_1 = line_swap(partial_2, 1)
    arrived_3 = exchange(picked_3, 1)
    grad_pieces = pick_grads(order, grads, after=[partial_2])
    (partial_3,) = products(arrived_3, after=grad_pieces[:1])
    partial_3, grad_pieces = lax.optimization_barrier((partial_3, grad_pieces))
    arrived_grads = exchange(grad_pieces, 1)
    inverse = newton(total, partial_3, from_1, from_2)

    inverse_1, inverse_2, inverse_3 = [line_swap(inverse, mask) for mask in (1, 2, 3)]
    made_a = apply((3, 2), [inverse, inverse_1], arrived_grads)
    result_a = exchange(made_a, -1)
    made_b = apply((1, 0), [inverse_2, inverse_3], arrived_grads, after=result_a[1:2])
    result_b = exchange(made_b, -1)
    partly = put_back(order, ((3, 2),), result_a)
    return put_back(order, ((1, 0),), result_b, partly)[None]


def solution(mesh):
    return jax.shard_map(
        shards,
        mesh=mesh,
        in_specs=(
            P("owner", ("member", "dp"), None),
            P("owner", None),
            P("owner", None, ("member", "dp")),
        ),
        out_specs=P("owner", None, ("member", "dp")),
        check_vma=False,
    )
```

```python
import functools

import jax
import jax.numpy as jnp
from jax import lax
from jax.experimental import pallas as pl
from jax.experimental.pallas import tpu as pltpu
from jax.sharding import PartitionSpec as P

BLK = 512
NS_STEPS = 12
DAMPING = 0.001
TILE = 128
LANES = 128
SIDE = BLK // TILE
UPPER = [(r, c) for r in range(SIDE) for c in range(r + 1, SIDE)]
DIAGONAL = [(r, r + 1) for r in range(0, SIDE, 2)]
TAIL = (len(UPPER) + len(DIAGONAL)) * TILE
PACKED = TAIL + 16
RING = 4
LINE = 4
UNROLL = 64
PHASES = (3, 2, 1, 0)

VMEM = pl.BlockSpec(memory_space=pltpu.VMEM)
SMEM = pl.BlockSpec(memory_space=pltpu.SMEM)
ANY = pl.BlockSpec(memory_space=pl.ANY)
PARAMS = pltpu.CompilerParams(vmem_limit_bytes=48 * 1024 * 1024)


def ring_shift(value, step):
    pairs = [
        (z * RING + x, z * RING + (x + step) % RING) for z in range(LINE) for x in range(RING)
    ]
    return lax.ppermute(value, "dp", pairs)


def line_swap(value, mask):
    pairs = [(z * RING + x, (z ^ mask) * RING + x) for z in range(LINE) for x in range(RING)]
    return lax.ppermute(value, "dp", pairs)


def block_start(phase, offset):
    place = lax.axis_index("dp")
    z = lax.div(place, RING)
    x = lax.rem(place, RING)
    block = lax.bitwise_xor(z, phase) * RING + lax.rem(x + offset, RING)
    return block * BLK


def gather_rows(order, start, sources, targets):
    def step(group, carry):
        first = pl.multiple_of(group * UNROLL, UNROLL)
        for inner in range(UNROLL):
            row = order[0, start + first + inner]
            for source, target in zip(sources, targets):
                target[pl.ds(first + inner, 1), :] = source[pl.ds(row, 1), :]
        return carry

    lax.fori_loop(0, BLK // UNROLL, step, 0)


def pick_columns_kernel(phases, order, rows, *refs):
    outs, turned, picked = refs[-RING - 4 : -4], refs[-4:-2], refs[-2:]
    width = 256
    for first in range(0, rows.shape[1], width):
        part = rows[:, first : first + width].astype(jnp.float32).T
        for half, target in enumerate(turned):
            target[first : first + width, :] = part[:, half * LANES : (half + 1) * LANES]
    filled = len(phases) * BLK
    for offset in range(RING):
        if outs[offset].shape[0] > filled:
            outs[offset][filled:, :] = jnp.zeros_like(outs[offset][filled:, :])
        for place, phase in enumerate(phases):
            gather_rows(order, block_start(phase, offset), turned, picked)
            for half, source in enumerate(picked):
                outs[offset][
                    place * BLK : (place + 1) * BLK, half * LANES : (half + 1) * LANES
                ] = source[...].astype(jnp.bfloat16)


def pick_columns(phases, order, rows, after=(), pad=0):
    tokens, features = rows.shape
    return pl.pallas_call(
        functools.partial(pick_columns_kernel, phases),
        out_shape=[jax.ShapeDtypeStruct((len(phases) * BLK + pad, tokens), jnp.bfloat16)] * RING,
        in_specs=[SMEM, VMEM] + [ANY] * len(after),
        out_specs=[VMEM] * RING,
        scratch_shapes=[pltpu.VMEM((features, LANES), jnp.float32)] * 2
        + [pltpu.VMEM((BLK, LANES), jnp.float32)] * 2,
        compiler_params=PARAMS,
        name="pick_columns",
    )(order, rows, *after)


def pick_grads_kernel(order, grads, *refs):
    outs, (wide, picked) = refs[-2 - RING : -2], refs[-2:]
    wide[...] = grads[...].astype(jnp.float32)
    for place, phase in enumerate(PHASES):
        for offset in range(RING):
            gather_rows(order, block_start(phase, offset), [wide], [picked])
            outs[offset][place * BLK : (place + 1) * BLK, :] = picked[...].astype(jnp.bfloat16)


def pick_grads(order, grads, after=()):
    features, columns = grads.shape
    return pl.pallas_call(
        pick_grads_kernel,
        out_shape=[jax.ShapeDtypeStruct((LINE * BLK, columns), jnp.bfloat16)] * RING,
        in_specs=[SMEM, VMEM] + [ANY] * len(after),
        out_specs=[VMEM] * RING,
        scratch_shapes=[
            pltpu.VMEM((features, columns), jnp.float32),
            pltpu.VMEM((BLK, columns), jnp.float32),
        ],
        compiler_params=PARAMS,
        name="pick_grads",
    )(order, grads, *after)


def tile_indices():
    rows = lax.broadcasted_iota(jnp.int32, (TILE, TILE), 0)
    columns = lax.broadcasted_iota(jnp.int32, (TILE, TILE), 1)
    return rows, columns


def pack(tile_at):
    rows, columns = tile_indices()
    parts = [tile_at(r, c) for r, c in UPPER]
    tails = []
    for first, second in DIAGONAL:
        other = tile_at(second, second)
        parts.append(jnp.where(columns >= rows, tile_at(first, first), other))
        tails.append(jnp.sum(jnp.where(rows == columns, other, 0.0), axis=0, keepdims=True))
    tails.append(jnp.zeros((PACKED - TAIL - len(tails), TILE), jnp.float32))
    return parts + [jnp.concatenate(tails, axis=0)]


def unpack(packed, target):
    rows, columns = tile_indices()

    def store(r, c, value):
        target[r * TILE : (r + 1) * TILE, c * TILE : (c + 1) * TILE] = value.astype(target.dtype)

    for place, (r, c) in enumerate(UPPER):
        value = packed(place * TILE, TILE)
        store(r, c, value)
        store(c, r, value.T)
    tails = packed(TAIL, PACKED - TAIL)
    for place, (first, second) in enumerate(DIAGONAL):
        value = packed((len(UPPER) + place) * TILE, TILE)
        turned = value.T
        store(first, first, jnp.where(columns >= rows, value, turned))
        upper = jnp.where(columns > rows, turned, tails[place : place + 1, :])
        store(second, second, jnp.where(columns < rows, value, upper))


def spans(refs, start, stop):
    size = refs[0].shape[0]
    while start < stop:
        index, first = divmod(start, size)
        length = min(stop - start, size - first)
        yield refs[index], first, length
        start += length


def store_parts(outs, parts, extra=()):
    start = 0
    for part in parts:
        stop = start + part.shape[0]
        taken = 0
        pieces = []
        if extra:
            for ref, first, length in spans(extra, start, stop):
                pieces.append((part[taken : taken + length, :] + ref[first : first + length, :]))
                taken += length
            part = pieces[0] if len(pieces) == 1 else jnp.concatenate(pieces, axis=0)
        taken = 0
        for ref, first, length in spans(outs, start, stop):
            ref[first : first + length, :] = part[taken : taken + length, :].astype(ref.dtype)
            taken += length
        start = stop


def products_kernel(adds, cuts, *refs):
    pieces, extra = refs[:RING], refs[RING : RING + adds]
    outs, joined = refs[-1 - cuts : -1], refs[-1]
    tokens = pieces[0].shape[1]
    for place, piece in enumerate(pieces):
        joined[:, place * tokens : (place + 1) * tokens] = piece[:BLK, :]
    strips = [
        lax.dot_general(
            joined[r * TILE : (r + 1) * TILE, :],
            joined[r * TILE :, :],
            (((1,), (1,)), ((), ())),
            preferred_element_type=jnp.float32,
        )
        for r in range(SIDE)
    ]
    parts = pack(lambda r, c: strips[r][:, (c - r) * TILE : (c - r + 1) * TILE])
    store_parts(outs, parts, extra)


def products(pieces, *extra, after=(), cuts=1):
    tokens = pieces[0].shape[1]
    return pl.pallas_call(
        functools.partial(products_kernel, len(extra), cuts),
        out_shape=[jax.ShapeDtypeStruct((PACKED // cuts, TILE), jnp.float32)] * cuts,
        in_specs=[VMEM] * (RING + len(extra)) + [ANY] * len(after),
        out_specs=[VMEM] * cuts,
        scratch_shapes=[pltpu.VMEM((BLK, RING * tokens), jnp.bfloat16)],
        compiler_params=PARAMS,
        name="products",
    )(*pieces, *extra, *after)


def halves(value):
    high = value.astype(jnp.bfloat16)
    low = (value - high.astype(jnp.float32)).astype(jnp.bfloat16)
    return high, low


def dot(left, right):
    return jnp.dot(left, right, preferred_element_type=jnp.float32)


def dot3(left, right):
    left_high, left_low = left
    right_high, right_low = right
    return dot(left_high, right_high) + (dot(left_high, right_low) + dot(left_low, right_high))


def newton_kernel(total, own, sibling, out, damped):
    rows = lax.broadcasted_iota(jnp.int32, (BLK, BLK), 0)
    columns = lax.broadcasted_iota(jnp.int32, (BLK, BLK), 1)
    identity = jnp.where(rows == columns, 1.0, 0.0).astype(jnp.float32)
    def packed(start, size):
        part = slice(start, start + size)
        return (own[part, :] + sibling[part, :]) / float(total)

    unpack(packed, damped)
    matrix = damped[...] + DAMPING * identity
    scale = 1.0 / jnp.max(jnp.sum(jnp.abs(matrix), axis=1, keepdims=True), axis=0, keepdims=True)
    matrix_parts = halves(matrix)
    approx = scale * (2.0 * identity - scale * matrix)

    def step(iteration, current):
        parts = halves(current)
        residual = identity - dot3(matrix_parts, parts)
        return current + dot3(parts, halves(residual))

    approx = lax.fori_loop(1, NS_STEPS, step, approx)
    store_parts(
        [out],
        pack(lambda r, c: approx[r * TILE : (r + 1) * TILE, c * TILE : (c + 1) * TILE]),
    )


def newton(total, own, sibling):
    return pl.pallas_call(
        functools.partial(newton_kernel, total),
        out_shape=jax.ShapeDtypeStruct((PACKED, TILE), jnp.bfloat16),
        in_specs=[VMEM] * 2,
        out_specs=VMEM,
        scratch_shapes=[pltpu.VMEM((BLK, BLK), jnp.float32)],
        compiler_params=PARAMS,
        name="newton",
    )(own, sibling)


def apply_kernel(places, waits, *refs):
    count = len(places)
    inverses, pieces = refs[:count], refs[count : count + RING]
    outs, (full, joined) = refs[count + RING + waits : -2], refs[-2:]
    columns = pieces[0].shape[1]
    for index, (place, inverse) in enumerate(zip(places, inverses)):
        unpack(lambda start, size: inverse[start : start + size, :].astype(jnp.float32), full)
        for offset, piece in enumerate(pieces):
            joined[:, offset * columns : (offset + 1) * columns] = piece[
                place * BLK : (place + 1) * BLK, :
            ]
        result = dot(full[...], joined[...]).astype(jnp.bfloat16)
        for offset in range(RING):
            outs[offset][index * BLK : (index + 1) * BLK, :] = result[
                :, offset * columns : (offset + 1) * columns
            ]
    if len(outs) > RING:
        outs[RING][...] = inverses[0][...]


def apply(places, inverses, pieces, after=(), forward=False):
    columns = pieces[0].shape[1]
    shapes = [jax.ShapeDtypeStruct((len(places) * BLK, columns), jnp.bfloat16)] * RING
    if forward:
        shapes.append(jax.ShapeDtypeStruct(inverses[0].shape, inverses[0].dtype))
    return pl.pallas_call(
        functools.partial(apply_kernel, places, len(after)),
        out_shape=shapes,
        in_specs=[VMEM] * (RING + len(places)) + [ANY] * len(after),
        out_specs=[VMEM] * len(shapes),
        scratch_shapes=[
            pltpu.VMEM((BLK, BLK), jnp.bfloat16),
            pltpu.VMEM((BLK, RING * columns), jnp.bfloat16),
        ],
        compiler_params=PARAMS,
        name="apply",
    )(*inverses, *pieces, *after)


def put_back_kernel(groups, last, order, *refs):
    pieces, refs = refs[: RING * len(groups)], refs[RING * len(groups) :]
    if last:
        before, out, wide, held = refs
        wide[...] = before[...]
    else:
        wide, held = refs
    for group, places in enumerate(groups):
        for index, place in enumerate(places):
            for offset in range(RING):
                start = block_start(PHASES[place], offset)
                piece = pieces[group * RING + offset]
                held[...] = piece[index * BLK : (index + 1) * BLK, :].astype(jnp.float32)

                def step(batch, carry):
                    first = pl.multiple_of(batch * UNROLL, UNROLL)
                    for inner in range(UNROLL):
                        row = order[0, start + first + inner]
                        wide[pl.ds(row, 1), :] = held[pl.ds(first + inner, 1), :]
                    return carry

                lax.fori_loop(0, BLK // UNROLL, step, 0)
    if last:
        out[...] = wide[...].astype(jnp.bfloat16)


def put_back(order, groups, pieces, before=None):
    columns = pieces[0].shape[1]
    features = order.shape[1]
    last = before is not None
    wide = pltpu.VMEM((features, columns), jnp.float32)
    held = pltpu.VMEM((BLK, columns), jnp.float32)
    return pl.pallas_call(
        functools.partial(put_back_kernel, groups, last),
        out_shape=jax.ShapeDtypeStruct(
            (features, columns), jnp.bfloat16 if last else jnp.float32
        ),
        in_specs=[SMEM] + [VMEM] * (len(pieces) + last),
        out_specs=VMEM,
        scratch_shapes=[wide, held] if last else [held],
        compiler_params=PARAMS,
        name="put_back",
    )(order, *pieces, *([before] if last else []))


def exchange(pieces, sign):
    return [pieces[0]] + [ring_shift(pieces[k], sign * k) for k in range(1, RING)]


def shards(factor_rows, feature_order, gradients):
    rows = factor_rows[0]
    grads = gradients[0]
    total = rows.shape[0] * lax.axis_size("dp")

    order = feature_order
    picked_0 = pick_columns(PHASES[:1], order, rows, pad=16)
    picked_1 = pick_columns(PHASES[1:2], order, rows, after=picked_0[:1], pad=16)
    arrived_0 = exchange(picked_0, 1)
    arrived_1 = exchange(picked_1, 1)
    partial_0 = products(arrived_0, after=picked_1[:1], cuts=2)
    picked_2 = pick_columns(PHASES[2:3], order, rows, after=partial_0[:1], pad=16)
    from_3 = [line_swap(half, 1) for half in partial_0]
    arrived_1, picked_2 = lax.optimization_barrier((arrived_1, picked_2))
    (partial_1,) = products(arrived_1, *from_3)
    from_2 = line_swap(partial_1, 2)
    arrived_2 = exchange(picked_2, 1)
    picked_3 = pick_columns(PHASES[3:], order, rows, after=[partial_1])
    (partial_2,) = products(arrived_2, after=picked_3[:1])
    from_1 = line_swap(partial_2, 1)
    arrived_3 = exchange(picked_3, 1)
    grad_pieces = pick_grads(order, grads, after=[partial_2])
    (partial_3,) = products(arrived_3, from_2, after=grad_pieces[:1])
    partial_3, grad_pieces = lax.optimization_barrier((partial_3, grad_pieces))
    arrived_grads = exchange(grad_pieces, 1)
    inverse = newton(total, partial_3, from_1)

    *made_0, inverse = apply((3,), [inverse], arrived_grads, forward=True)
    inverse_1, inverse_2 = [line_swap(inverse, mask) for mask in (1, 2)]
    result_0 = exchange(made_0, -1)
    made_1 = list(apply((2,), [inverse_1], arrived_grads, after=result_0[1:]))
    result_1 = exchange(made_1, -1)
    inverse_2, made_1[0] = lax.optimization_barrier((inverse_2, made_1[0]))
    inverse_3 = line_swap(inverse_2, 1)
    made_2 = apply((1,), [inverse_2], arrived_grads, after=made_1[:1])
    result_2 = exchange(made_2, -1)
    made_3 = apply((0,), [inverse_3], arrived_grads, after=(made_2[0], *result_1[1:]))
    result_3 = exchange(made_3, -1)
    partly = put_back(order, ((3,), (2,), (1,)), result_0 + result_1 + result_2)
    return put_back(order, ((0,),), result_3, partly)[None]


def solution(mesh):
    return jax.shard_map(
        shards,
        mesh=mesh,
        in_specs=(
            P("owner", ("member", "dp"), None),
            P("owner", None),
            P("owner", None, ("member", "dp")),
        ),
        out_specs=P("owner", None, ("member", "dp")),
        check_vma=False,
    )
```
